32 devices in a mesh: seg: 16 (over z, y, x), tp: 2 (over core).
Axes of the slice: x: 2, y: 2, z: 4, core: 2. Of those that a mesh axis runs over, the one named last changes fastest.
Arguments:
- qkv: bfloat16 [3, 6144, 6144], P(None, 'seg', 'tp'), may hold values from -20 to 20
- note_slot_document: int32 [48], replicated, may hold values from 0 to 7, never falling along the last dimension, each value on 1 to 9 neighbouring positions
- note_rows: int32 [48], replicated, may hold values from 2 to 128, as said below
- out_weight: bfloat16 [6144, 6144], P('seg', 'tp'), may hold values from -0.3125 to 0.3125
Outputs:
- attended: bfloat16 [6144, 6144], P('seg', 'tp')
The draws below stay inside these ranges and needn't reach their ends.
Inputs may be any that keep to these rules, and one draw needn't show every extreme that they name: `note_slot_document`: slot ids never fall, a document holds 1 to 9 consecutive slots. `note_rows`: live rows of a block come first.
All inputs are finite; a program needn't handle non-finite values.
Results may differ from the reference program's by a relative error of at most 0.014.
Values may be sent and summed in bfloat16 or wider, within the bound.
A program may use at most 128 MiB of HBM per device.

```python
import math
import jax
import jax.numpy as jnp
import numpy as np
from jax import lax

D = 6144
DH = 128
NOTE_BLOCK_ROWS = 128
SEG = 384
HD = 6144
SEGMENT_SLOTS = 3
TOTAL_NOTE_SLOTS = 48
TOKENS = 6144
N_SEG = 16


def draw_qkv(key, part):
    parts_key = jax.random.split(key, 2)
    base = jnp.clip(jax.random.normal(parts_key[0], (3, TOKENS, HD), jnp.float32), -4.0, 4.0)
    row_scale = jnp.exp(jax.random.uniform(parts_key[1], (2, TOKENS, 1), jnp.float32, math.log(0.3), math.log(3.0)))
    queries = base[0] * row_scale[0]
    key_rows = base[1] * row_scale[1]
    value_rows = base[2] * 3.0
    return jnp.stack([queries, key_rows, value_rows]).astype(jnp.bfloat16)


def draw_note_rows(key, part):
    block_tallies = jax.random.randint(jax.random.fold_in(key, 11), (TOTAL_NOTE_SLOTS,), 2, NOTE_BLOCK_ROWS + 1)
    picked_blocks = jax.random.randint(jax.random.fold_in(key, 12), (), 0, TOTAL_NOTE_SLOTS)
    return jnp.where(jnp.arange(TOTAL_NOTE_SLOTS) == picked_blocks, NOTE_BLOCK_ROWS, block_tallies).astype(jnp.int32)


def shard_levels(own_key, shape, cuts, least, largest):
    level = 1.0
    for position, shards_of in cuts:
        steps = jax.random.uniform(jax.random.fold_in(jax.random.fold_in(own_key, 6), position), (shards_of,), jnp.float32, least / len(cuts), largest / len(cuts))
        level = level * jnp.repeat(jnp.exp(steps), shape[position] // shards_of).reshape((-1,) + (1,) * (len(shape) - 1 - position))
    return level


def length_profile(number_of, total, limit, skew):
    portions = [(1 << 20) // math.isqrt(rank ** skew) + 1 for rank in range(2, number_of + 1)]
    rest, counts = total - limit - (number_of - 1), [1] * (number_of - 1)
    while rest > 0:
        movable = [i for i in range(number_of - 1) if counts[i] < limit]
        mass, left = sum([portions[i] for i in movable]), rest
        for i in movable:
            addition = min(limit - counts[i], max(1, left * portions[i] // mass), rest)
            counts[i] = counts[i] + addition
            rest = rest - addition
    return np.array([limit] + counts)


def uneven_parts(stream_key, number_of, total, reach, skew):
    if number_of == 2:
        one = jax.random.randint(stream_key, (), max(1, total - reach), min(reach, total - 1) + 1)
        return jnp.stack([one, total - one])
    tallies = jnp.asarray(length_profile(number_of, total, reach, skew), jnp.int32)
    pairs = (number_of - 1) // 2
    donor, taker = tallies[1:1 + 2 * pairs:2], tallies[2:2 + 2 * pairs:2]
    margin = jnp.minimum(donor - 1, reach - taker)
    moved = jax.random.randint(jax.random.fold_in(stream_key, 1), (pairs,), 0, 1 << 20) % (margin + 1)
    tallies = tallies.at[1:1 + 2 * pairs:2].set(donor - moved).at[2:2 + 2 * pairs:2].set(taker + moved)
    return tallies[jax.random.permutation(jax.random.fold_in(stream_key, 2), number_of)]


def normal_values(stream_key, shape, width, limit, pieces=(), kind=jnp.bfloat16):
    array = jax.random.normal(stream_key, shape, jnp.float32) * width
    if len(pieces) > 0:
        array = shard_levels(stream_key, shape, pieces, -0.22, 0.18) * array
    return jnp.clip(array, min=-limit, max=limit).astype(kind)


def setup_inputs(seed: int = 0) -> dict:
    streams_of = jax.random.split(jax.random.key(seed), 5)
    qkv = draw_qkv(jax.random.fold_in(streams_of[4], 71), 0)
    note_slot_document = jnp.searchsorted(jnp.cumsum(uneven_parts(streams_of[1], N_SEG // 2, TOTAL_NOTE_SLOTS, 3 * SEGMENT_SLOTS, 1)), jnp.arange(TOTAL_NOTE_SLOTS), side="right").astype(jnp.int32)
    note_rows = draw_note_rows(jax.random.fold_in(streams_of[4], 71), 0)
    out_weight = normal_values(streams_of[3], (HD, D), (HD // 16) ** -0.5, 0.3125, ((0, 16), (1, 2)))
    return dict(qkv=qkv, note_slot_document=note_slot_document, note_rows=note_rows, out_weight=out_weight)


masked_score = -1e30


def attend(queries, key_rows, value_rows, query_doc, key_doc):
    scores = jnp.einsum("qhd,khd->hqk", queries.astype(jnp.float32), key_rows.astype(jnp.float32)) * (DH ** -0.5)
    scores = jnp.where((query_doc[:, None] == key_doc[None, :])[None], scores, masked_score)
    row_max = jnp.max(scores, axis=-1, keepdims=True)
    exponent = jnp.exp(scores - row_max)
    weights = (exponent / jnp.sum(exponent, axis=-1, keepdims=True)).astype(jnp.bfloat16)
    mixed = jnp.einsum("hqk,khd->qhd", weights.astype(jnp.float32), value_rows.astype(jnp.float32))
    return mixed.astype(jnp.bfloat16)


def reference(qkv, note_slot_document, note_rows, out_weight):
    head_count = HD // DH
    inside_note_block = jnp.arange(SEG) % NOTE_BLOCK_ROWS

    def one_segment(segment_index):
        first_row = (segment_index * SEG).astype(jnp.int32)
        past_index = jnp.maximum(segment_index - 1, 0).astype(jnp.int32)
        own_block = lax.dynamic_slice_in_dim(qkv, first_row, SEG, 1)
        past_block = lax.dynamic_slice_in_dim(qkv, (past_index * SEG).astype(jnp.int32), SEG, 1)
        slot_docs = lax.dynamic_slice_in_dim(note_slot_document, (segment_index * SEGMENT_SLOTS).astype(jnp.int32), SEGMENT_SLOTS)
        slot_live = lax.dynamic_slice_in_dim(note_rows, (segment_index * SEGMENT_SLOTS).astype(jnp.int32), SEGMENT_SLOTS)
        past_docs = lax.dynamic_slice_in_dim(note_slot_document, (past_index * SEGMENT_SLOTS).astype(jnp.int32), SEGMENT_SLOTS)
        past_docs = jnp.where(segment_index > 0, past_docs, -1)
        past_live = lax.dynamic_slice_in_dim(note_rows, (past_index * SEGMENT_SLOTS).astype(jnp.int32), SEGMENT_SLOTS)
        row_docs = jnp.repeat(slot_docs, NOTE_BLOCK_ROWS)
        own_doc = jnp.where(inside_note_block < jnp.repeat(slot_live, NOTE_BLOCK_ROWS), row_docs, -2)
        earlier_document = jnp.where(inside_note_block < jnp.repeat(past_live, NOTE_BLOCK_ROWS), jnp.repeat(past_docs, NOTE_BLOCK_ROWS), -2)
        queries = own_block[0].reshape(SEG, head_count, DH)
        key_rows = jnp.concatenate([past_block[1], own_block[1]], axis=0).reshape(2 * SEG, head_count, DH)
        value_rows = jnp.concatenate([past_block[2], own_block[2]], axis=0).reshape(2 * SEG, head_count, DH)
        mixed = attend(queries, key_rows, value_rows, row_docs, jnp.concatenate([earlier_document, own_doc]))
        return jnp.dot(mixed.reshape(SEG, HD), out_weight, preferred_element_type=jnp.float32).astype(jnp.bfloat16)

    projected = lax.map(one_segment, jnp.arange(N_SEG, dtype=jnp.int32))
    return projected.reshape(TOKENS, D)
```

```python
import jax
import jax.numpy as jnp
from jax import lax
from jax.experimental import pallas as pl
from jax.experimental.pallas import tpu as pltpu
from jax.sharding import PartitionSpec as P

DH = 128
NOTE_BLOCK_ROWS = 128


masked_score = -1e30


def from_behind(x, axis, by):
    length = lax.axis_size(axis)
    pairs = [(i, i + by) for i in range(length) if 0 <= i + by < length]
    return lax.ppermute(x, axis, pairs)


def attend(queries, key_rows, value_rows, query_doc, key_doc):
    scores = jnp.einsum(
        "qhd,khd->hqk", queries, key_rows, preferred_element_type=jnp.float32
    ) * DH ** (-0.5)
    scores = jnp.where((query_doc[:, None] == key_doc[None, :])[None], scores, masked_score)
    row_max = jnp.max(scores, axis=-1, keepdims=True)
    exponent = jnp.exp(scores - row_max)
    weights = (exponent / jnp.sum(exponent, axis=-1, keepdims=True)).astype(jnp.bfloat16)
    mixed = jnp.einsum("hqk,khd->qhd", weights, value_rows, preferred_element_type=jnp.float32)
    return mixed.astype(jnp.bfloat16)


def attend_blocks(queries, key_rows, value_rows, row_docs, key_doc):
    row_count, head_count = (queries.shape[0], queries.shape[1])
    block_rows = min(row_count, 512)
    block_count = row_count // block_rows

    def one_block(query_pair):
        return attend(query_pair[0], key_rows, value_rows, query_pair[1], key_doc)

    mixed = lax.map(
        one_block,
        (
            queries.reshape(block_count, block_rows, head_count, DH),
            row_docs.reshape(block_count, block_rows),
        ),
    )
    return mixed.reshape(row_count, head_count * DH)


def shards(qkv, note_slot_document, note_rows, out_weight):
    row_count = qkv.shape[1]
    head_count = qkv.shape[2] // DH
    slot_count = row_count // NOTE_BLOCK_ROWS
    seg_place = lax.axis_index("seg")
    memory = from_behind(qkv[1:], "seg", 1)
    slot_docs = lax.dynamic_slice_in_dim(note_slot_document, seg_place * slot_count, slot_count)
    slot_live = lax.dynamic_slice_in_dim(note_rows, seg_place * slot_count, slot_count)
    past_first = jnp.maximum(seg_place - 1, 0) * slot_count
    past_docs = jnp.where(
        seg_place > 0, lax.dynamic_slice_in_dim(note_slot_document, past_first, slot_count), -1
    )
    past_live = lax.dynamic_slice_in_dim(note_rows, past_first, slot_count)
    inside_note_block = jnp.arange(row_count) % NOTE_BLOCK_ROWS
    row_docs = jnp.repeat(slot_docs, NOTE_BLOCK_ROWS)
    own_doc = jnp.where(inside_note_block < jnp.repeat(slot_live, NOTE_BLOCK_ROWS), row_docs, -2)
    earlier_document = jnp.where(
        inside_note_block < jnp.repeat(past_live, NOTE_BLOCK_ROWS),
        jnp.repeat(past_docs, NOTE_BLOCK_ROWS),
        -2,
    )
    queries = qkv[0].reshape(row_count, head_count, DH)
    own_keys = qkv[1].reshape(row_count, head_count, DH)
    own_values = qkv[2].reshape(row_count, head_count, DH)
    key_rows = jnp.concatenate([memory[0].reshape(row_count, head_count, DH), own_keys], axis=0)
    value_rows = jnp.concatenate([memory[1].reshape(row_count, head_count, DH), own_values], axis=0)
    mixed_heads = attend_blocks(
        queries, key_rows, value_rows, row_docs, jnp.concatenate([earlier_document, own_doc])
    )
    heads_all = lax.all_gather(mixed_heads, "tp", axis=1, tiled=True)
    summed = jnp.dot(
        heads_all,
        lax.all_gather(out_weight, "seg", axis=0, tiled=True),
        preferred_element_type=jnp.float32,
    )
    return summed.astype(jnp.bfloat16)


PLANE = 4
LINE = 4
CHUNKS = 4
LOG2_E = 1.4426950408889634
MESH = pl.DeviceIdType.MESH


def fused(
    docs, live, qkv, w, out, x, wv, mixed, bias, give, take, kept, done,
    x_send, x_recv, halo_send, halo_recv, w_send, w_recv, core_send, core_recv,
    sum_send, sum_recv, own_sem, out_sem,
):
    seg, tp = lax.axis_index("seg"), lax.axis_index("tp")
    z, k = seg // PLANE, seg % PLANE
    kx, ky = k % 2, k // 2
    rows = qkv.shape[1]
    width = w.shape[1] // CHUNKS
    group = w.shape[0]
    heads = group // DH
    slots = rows // NOTE_BLOCK_ROWS
    inner = jnp.logical_and(z > 0, z < LINE - 1)

    def mate(m):
        px = 1 - kx if m in (1, 3) else kx
        py = 1 - ky if m in (2, 3) else ky
        return 2 * py + px

    def at(zz, kk, cc=None):
        return (zz * PLANE + kk, tp if cc is None else cc)

    barrier = pltpu.get_barrier_semaphore()
    peers = [at(z, mate(m)) for m in (1, 2, 3)]
    peers += [at((z + d) % LINE, k) for d in (1, 2, 3)] + [at(z, k, 1 - tp)]
    for peer in peers:
        pl.semaphore_signal(barrier, inc=1, device_id=peer, device_id_type=MESH)
    pl.semaphore_wait(barrier, len(peers))

    def x_copy(t, m):
        return pltpu.make_async_remote_copy(
            src_ref=qkv.at[:, :, pl.ds(pl.multiple_of((PLANE * t + mate(m)) * group, DH), group)],
            dst_ref=x.at[t, k + 1],
            send_sem=x_send.at[t, m],
            recv_sem=x_recv.at[t, m],
            device_id=at(z, mate(m)),
            device_id_type=MESH,
        )

    def x_own(t):
        return pltpu.make_async_copy(
            qkv.at[:, :, pl.ds(pl.multiple_of((PLANE * t + k) * group, DH), group)],
            x.at[t, k + 1],
            x_recv.at[t, 0],
        )

    def halo_copy(t):
        return pltpu.make_async_remote_copy(
            src_ref=x.at[t, PLANE, pl.ds(1, 2)],
            dst_ref=x.at[t, 0, pl.ds(1, 2)],
            send_sem=halo_send.at[t],
            recv_sem=halo_recv.at[t],
            device_id=at(jnp.minimum(z + 1, LINE - 1), k),
            device_id_type=MESH,
        )

    def w_block(zz, n):
        return wv.at[pl.ds(pl.multiple_of(zz * group, DH), group), pl.ds(n * width, width)]

    def w_copy(slot, step, n):
        return pltpu.make_async_remote_copy(
            src_ref=w.at[:, pl.ds(n * width, width)],
            dst_ref=w_block(z, n),
            send_sem=w_send.at[slot, n],
            recv_sem=w_recv.at[z, n],
            device_id=at(z + step, k),
            device_id_type=MESH,
        )

    def w_relay(n):
        far = 6 - 3 * z
        return pltpu.make_async_remote_copy(
            src_ref=w_block(far, n),
            dst_ref=w_block(far, n),
            send_sem=w_send.at[4, n],
            recv_sem=w_recv.at[far, n],
            device_id=at(3 * z - 3, k),
            device_id_type=MESH,
        )

    def w_own(n):
        return pltpu.make_async_copy(
            w.at[:, pl.ds(n * width, width)], w_block(z, n), own_sem.at[n]
        )

    def w_arrived(zz, n):
        pltpu.make_async_copy(w_block(zz, n), w_block(zz, n), w_recv.at[zz, n]).wait()

    w_steps = ((0, 2), (1, -2), (2, 1), (3, -1))

    def reaches(step):
        return z < LINE - step if step > 0 else z >= -step

    for t in range(2):
        for m in (3, 1, 2):
            x_copy(t, m).start()
        x_own(t).start()
    for n in range(CHUNKS):
        for slot, step in w_steps:
            @pl.when(reaches(step))
            def _():
                w_copy(slot, step, n).start()
        w_own(n).start()

    @pl.when(z == 0)
    def _():
        for t in range(2):
            x[t, 0, 1:3] = jnp.zeros((2, rows, group), x.dtype)

    place = lax.broadcasted_iota(jnp.int32, (NOTE_BLOCK_ROWS, NOTE_BLOCK_ROWS), 1)

    @pl.loop(0, PLANE)
    def _(j):
        first = (z * PLANE + j) * slots
        for a in range(slots):
            for b in range(2 * slots):
                key_slot = first + b - slots
                safe = jnp.maximum(key_slot, 0)
                same = jnp.logical_and(docs[safe] == docs[first + a], key_slot >= 0)
                limit = jnp.where(same, live[safe], 0)
                bias[
                    j,
                    a * NOTE_BLOCK_ROWS : (a + 1) * NOTE_BLOCK_ROWS,
                    b * NOTE_BLOCK_ROWS : (b + 1) * NOTE_BLOCK_ROWS,
                ] = jnp.where(place < limit, 0.0, masked_score)

    def attend_rows(t, j):
        for h in range(heads):
            lanes = slice(h * DH, (h + 1) * DH)
            q = x[t, j + 1, 0, :, lanes]
            scores = [
                lax.dot_general(
                    q,
                    x[t, j + i, 1, :, lanes],
                    (((1,), (1,)), ((), ())),
                    preferred_element_type=jnp.float32,
                )
                * (DH ** (-0.5) * LOG2_E)
                + bias[j, :, i * rows : (i + 1) * rows]
                for i in range(2)
            ]
            top = jnp.max(jnp.maximum(scores[0], scores[1]), axis=-1, keepdims=True)
            powers = [jnp.exp2(s - top) for s in scores]
            total = jnp.sum(powers[0] + powers[1], axis=-1, keepdims=True)
            value = sum(
                jnp.dot(
                    powers[i].astype(jnp.bfloat16),
                    x[t, j + i, 2, :, lanes],
                    preferred_element_type=jnp.float32,
                )
                for i in range(2)
            )
            column = pl.multiple_of((2 * tp + t) * group + h * DH, DH)
            mixed[j, :, pl.ds(column, DH)] = (value / total).astype(jnp.bfloat16)

    def core_copy(t, j):
        part = mixed.at[j, :, pl.ds(pl.multiple_of((2 * tp + t) * group, DH), group)]
        return pltpu.make_async_remote_copy(
            src_ref=part,
            dst_ref=part,
            send_sem=core_send.at[t, j],
            recv_sem=core_recv.at[t, j],
            device_id=at(z, k, 1 - tp),
            device_id_type=MESH,
        )

    def relay(n):
        @pl.when(inner)
        def _():
            w_arrived(6 - 3 * z, n)
            w_relay(n).start()

    for t in range(2):
        x_own(t).wait()
        for m in (1, 2, 3):
            x_copy(t, m).wait_recv()

        @pl.when(z < LINE - 1)
        def _():
            halo_copy(t).start()

        relay(t)

        @pl.loop(1, PLANE)
        def _(j):
            attend_rows(t, j)
            core_copy(t, j).start()

    relay(2)
    for t in range(2):
        @pl.when(z > 0)
        def _():
            halo_copy(t).wait_recv()

        attend_rows(t, 0)
        core_copy(t, 0).start()

    for t in range(2):
        for j in range(PLANE):
            core_copy(t, j).wait_recv()

    def sum_copy(m, n):
        return pltpu.make_async_remote_copy(
            src_ref=give.at[m - 1, n],
            dst_ref=take.at[m - 1, n],
            send_sem=sum_send.at[m - 1, n],
            recv_sem=sum_recv.at[m - 1, n],
            device_id=at(z, mate(m)),
            device_id_type=MESH,
        )

    for n in range(CHUNKS):
        w_own(n).wait()
        for zz in range(LINE):
            waited = jnp.logical_and(inner, 6 - 3 * z == zz)
            @pl.when(jnp.logical_and(z != zz, jnp.logical_not(waited)))
            def _():
                w_arrived(zz, n)
        for m in (3, 1, 2, 0):
            product = jnp.dot(
                mixed[mate(m)],
                wv[:, n * width : (n + 1) * width],
                preferred_element_type=jnp.float32,
            )
            if m == 0:
                kept[n] = product
            else:
                give[m - 1, n] = product.astype(jnp.bfloat16)
                sum_copy(m, n).start()
        if n == 1:
            relay(3)

    def out_copy(n):
        return pltpu.make_async_copy(
            done.at[n], out.at[:, pl.ds(n * width, width)], out_sem.at[n]
        )

    for n in range(CHUNKS):
        for m in (1, 2, 3):
            sum_copy(m, n).wait_recv()
        total = kept[n]
        for m in (1, 2, 3):
            total = total + take[m - 1, n].astype(jnp.float32)
        done[n] = total.astype(jnp.bfloat16)
        out_copy(n).start()

    for t in range(2):
        for m in (1, 2, 3):
            x_copy(t, m).wait_send()
        for j in range(PLANE):
            core_copy(t, j).wait_send()

        @pl.when(z < LINE - 1)
        def _():
            halo_copy(t).wait_send()

    for n in range(CHUNKS):
        for slot, step in w_steps:
            @pl.when(reaches(step))
            def _():
                w_copy(slot, step, n).wait_send()

        @pl.when(inner)
        def _():
            w_relay(n).wait_send()

        for m in (1, 2, 3):
            sum_copy(m, n).wait_send()
        out_copy(n).wait()


def fused_shards(qkv, note_slot_document, note_rows, out_weight):
    rows, group = qkv.shape[1], out_weight.shape[0]
    columns = out_weight.shape[1]
    width = columns // CHUNKS
    dma = pltpu.SemaphoreType.DMA
    anywhere = pl.BlockSpec(memory_space=pl.ANY)
    scalars = pl.BlockSpec(memory_space=pltpu.SMEM)
    return pl.pallas_call(
        fused,
        out_shape=jax.ShapeDtypeStruct((rows, columns), jnp.bfloat16),
        in_specs=[scalars, scalars, anywhere, anywhere],
        out_specs=anywhere,
        scratch_shapes=[
            pltpu.VMEM((2, PLANE + 1, 3, rows, group), jnp.bfloat16),
            pltpu.VMEM((LINE * group, columns), jnp.bfloat16),
            pltpu.VMEM((PLANE, rows, LINE * group), jnp.bfloat16),
            pltpu.VMEM((PLANE, rows, 2 * rows), jnp.float32),
            pltpu.VMEM((3, CHUNKS, rows, width), jnp.bfloat16),
            pltpu.VMEM((3, CHUNKS, rows, width), jnp.bfloat16),
            pltpu.VMEM((CHUNKS, rows, width), jnp.float32),
            pltpu.VMEM((CHUNKS, rows, width), jnp.bfloat16),
            dma((2, 4)), dma((2, 4)), dma((2,)), dma((2,)),
            dma((5, CHUNKS)), dma((LINE, CHUNKS)), dma((2, PLANE)), dma((2, PLANE)),
            dma((3, CHUNKS)), dma((3, CHUNKS)), dma((CHUNKS,)), dma((CHUNKS,)),
        ],
        compiler_params=pltpu.CompilerParams(
            collective_id=0, has_side_effects=True, vmem_limit_bytes=60 * 2**20
        ),
        cost_estimate=pl.CostEstimate(
            flops=2 * PLANE * rows * LINE * group * columns + 16 * rows * rows * DH * PLANE * 2 * group // DH,
            bytes_accessed=4 * (qkv.size + 3 * out_weight.size),
            transcendentals=PLANE * rows * 2 * rows * 2 * group // DH,
        ),
    )(note_slot_document, note_rows, qkv, out_weight)


def solution(mesh):
    in_specs = (P(None, "seg", "tp"), P(), P(), P("seg", "tp"))
    out_specs = P("seg", "tp")
    in_planes = mesh.shape["seg"] == PLANE * LINE and mesh.shape["tp"] == 2
    body = fused_shards if in_planes else shards
    return jax.shard_map(body, mesh=mesh, in_specs=in_specs, out_specs=out_specs, check_vma=False)
```

```python
import jax
import jax.numpy as jnp
from jax import lax
from jax.experimental import pallas as pl
from jax.experimental.pallas import tpu as pltpu
from jax.sharding import PartitionSpec as P

DH = 128
NOTE_BLOCK_ROWS = 128


masked_score = -1e30


def from_behind(x, axis, by):
    length = lax.axis_size(axis)
    pairs = [(i, i + by) for i in range(length) if 0 <= i + by < length]
    return lax.ppermute(x, axis, pairs)


def attend(queries, key_rows, value_rows, query_doc, key_doc):
    scores = jnp.einsum(
        "qhd,khd->hqk", queries, key_rows, preferred_element_type=jnp.float32
    ) * DH ** (-0.5)
    scores = jnp.where((query_doc[:, None] == key_doc[None, :])[None], scores, masked_score)
    row_max = jnp.max(scores, axis=-1, keepdims=True)
    exponent = jnp.exp(scores - row_max)
    weights = (exponent / jnp.sum(exponent, axis=-1, keepdims=True)).astype(jnp.bfloat16)
    mixed = jnp.einsum("hqk,khd->qhd", weights, value_rows, preferred_element_type=jnp.float32)
    return mixed.astype(jnp.bfloat16)


def attend_blocks(queries, key_rows, value_rows, row_docs, key_doc):
    row_count, head_count = (queries.shape[0], queries.shape[1])
    block_rows = min(row_count, 512)
    block_count = row_count // block_rows

    def one_block(query_pair):
        return attend(query_pair[0], key_rows, value_rows, query_pair[1], key_doc)

    mixed = lax.map(
        one_block,
        (
            queries.reshape(block_count, block_rows, head_count, DH),
            row_docs.reshape(block_count, block_rows),
        ),
    )
    return mixed.reshape(row_count, head_count * DH)


def shards(qkv, note_slot_document, note_rows, out_weight):
    row_count = qkv.shape[1]
    head_count = qkv.shape[2] // DH
    slot_count = row_count // NOTE_BLOCK_ROWS
    seg_place = lax.axis_index("seg")
    memory = from_behind(qkv[1:], "seg", 1)
    slot_docs = lax.dynamic_slice_in_dim(note_slot_document, seg_place * slot_count, slot_count)
    slot_live = lax.dynamic_slice_in_dim(note_rows, seg_place * slot_count, slot_count)
    past_first = jnp.maximum(seg_place - 1, 0) * slot_count
    past_docs = jnp.where(
        seg_place > 0, lax.dynamic_slice_in_dim(note_slot_document, past_first, slot_count), -1
    )
    past_live = lax.dynamic_slice_in_dim(note_rows, past_first, slot_count)
    inside_note_block = jnp.arange(row_count) % NOTE_BLOCK_ROWS
    row_docs = jnp.repeat(slot_docs, NOTE_BLOCK_ROWS)
    own_doc = jnp.where(inside_note_block < jnp.repeat(slot_live, NOTE_BLOCK_ROWS), row_docs, -2)
    earlier_document = jnp.where(
        inside_note_block < jnp.repeat(past_live, NOTE_BLOCK_ROWS),
        jnp.repeat(past_docs, NOTE_BLOCK_ROWS),
        -2,
    )
    queries = qkv[0].reshape(row_count, head_count, DH)
    own_keys = qkv[1].reshape(row_count, head_count, DH)
    own_values = qkv[2].reshape(row_count, head_count, DH)
    key_rows = jnp.concatenate([memory[0].reshape(row_count, head_count, DH), own_keys], axis=0)
    value_rows = jnp.concatenate([memory[1].reshape(row_count, head_count, DH), own_values], axis=0)
    mixed_heads = attend_blocks(
        queries, key_rows, value_rows, row_docs, jnp.concatenate([earlier_document, own_doc])
    )
    heads_all = lax.all_gather(mixed_heads, "tp", axis=1, tiled=True)
    summed = jnp.dot(
        heads_all,
        lax.all_gather(out_weight, "seg", axis=0, tiled=True),
        preferred_element_type=jnp.float32,
    )
    return summed.astype(jnp.bfloat16)


PLANE = 4
LINE = 4
CHUNKS = 6
LOG2_E = 1.4426950408889634
MESH = pl.DeviceIdType.MESH


def fused(
    docs, live, qkv, w, out, x, wv, mixed, bias, give, take, passed, landed, kept, later, done,
    x_send, x_recv, halo_send, halo_recv, w_send, w_recv, core_send, core_recv,
    give_send, give_recv, pass_send, pass_recv, own_sem, out_sem,
):
    seg, tp = lax.axis_index("seg"), lax.axis_index("tp")
    z, k = seg // PLANE, seg % PLANE
    kx, ky = k % 2, k // 2
    rows = qkv.shape[1]
    width = w.shape[1] // CHUNKS
    group = w.shape[0]
    heads = group // DH
    slots = rows // NOTE_BLOCK_ROWS
    inner = jnp.logical_and(z > 0, z < LINE - 1)

    def mate(m):
        px = 1 - kx if m in (1, 3) else kx
        py = 1 - ky if m in (2, 3) else ky
        return 2 * py + px

    def at(zz, kk, cc=None):
        return (zz * PLANE + kk, tp if cc is None else cc)

    barrier = pltpu.get_barrier_semaphore()
    peers = [at(z, mate(m)) for m in (1, 2, 3)]
    peers += [at((z + d) % LINE, k) for d in (1, 2, 3)] + [at(z, k, 1 - tp)]
    for peer in peers:
        pl.semaphore_signal(barrier, inc=1, device_id=peer, device_id_type=MESH)
    pl.semaphore_wait(barrier, len(peers))

    def x_copy(t, m):
        return pltpu.make_async_remote_copy(
            src_ref=qkv.at[:, :, pl.ds(pl.multiple_of((PLANE * t + mate(m)) * group, DH), group)],
            dst_ref=x.at[t, k + 1],
            send_sem=x_send.at[t, m],
            recv_sem=x_recv.at[t, m],
            device_id=at(z, mate(m)),
            device_id_type=MESH,
        )

    def x_own(t):
        return pltpu.make_async_copy(
            qkv.at[:, :, pl.ds(pl.multiple_of((PLANE * t + k) * group, DH), group)],
            x.at[t, k + 1],
            x_recv.at[t, 0],
        )

    def halo_copy(t):
        return pltpu.make_async_remote_copy(
            src_ref=x.at[t, PLANE, pl.ds(1, 2)],
            dst_ref=x.at[t, 0, pl.ds(1, 2)],
            send_sem=halo_send.at[t],
            recv_sem=halo_recv.at[t],
            device_id=at(jnp.minimum(z + 1, LINE - 1), k),
            device_id_type=MESH,
        )

    def w_block(zz, n):
        return wv.at[pl.ds(pl.multiple_of(zz * group, DH), group), pl.ds(n * width, width)]

    def w_copy(slot, step, n):
        return pltpu.make_async_remote_copy(
            src_ref=w.at[:, pl.ds(n * width, width)],
            dst_ref=w_block(z, n),
            send_sem=w_send.at[slot, n],
            recv_sem=w_recv.at[z, n],
            device_id=at(z + step, k),
            device_id_type=MESH,
        )

    def w_relay(n):
        far = 6 - 3 * z
        return pltpu.make_async_remote_copy(
            src_ref=w_block(far, n),
            dst_ref=w_block(far, n),
            send_sem=w_send.at[4, n],
            recv_sem=w_recv.at[far, n],
            device_id=at(3 * z - 3, k),
            device_id_type=MESH,
        )

    def w_own(n):
        return pltpu.make_async_copy(
            w.at[:, pl.ds(n * width, width)], w_block(z, n), own_sem.at[n]
        )

    def w_arrived(zz, n):
        pltpu.make_async_copy(w_block(zz, n), w_block(zz, n), w_recv.at[zz, n]).wait()

    w_steps = ((0, 2), (1, -2), (2, 1), (3, -1))

    def reaches(step):
        return z < LINE - step if step > 0 else z >= -step

    for t in range(2):
        for m in (3, 1, 2):
            x_copy(t, m).start()
        x_own(t).start()

    def w_start(n):
        for slot, step in w_steps:
            @pl.when(reaches(step))
            def _():
                w_copy(slot, step, n).start()

    w_start(0)
    w_start(1)
    for n in range(CHUNKS):
        w_own(n).start()

    @pl.when(z == 0)
    def _():
        for t in range(2):
            x[t, 0, 1:3] = jnp.zeros((2, rows, group), x.dtype)

    place = lax.broadcasted_iota(jnp.int32, (NOTE_BLOCK_ROWS, NOTE_BLOCK_ROWS), 1)

    @pl.loop(0, PLANE)
    def _(j):
        first = (z * PLANE + j) * slots
        for a in range(slots):
            for b in range(2 * slots):
                key_slot = first + b - slots
                safe = jnp.maximum(key_slot, 0)
                same = jnp.logical_and(docs[safe] == docs[first + a], key_slot >= 0)
                limit = jnp.where(same, live[safe], 0)
                bias[
                    j,
                    a * NOTE_BLOCK_ROWS : (a + 1) * NOTE_BLOCK_ROWS,
                    b * NOTE_BLOCK_ROWS : (b + 1) * NOTE_BLOCK_ROWS,
                ] = jnp.where(place < limit, 0.0, masked_score)

    def attend_rows(t, j):
        for h in range(heads):
            lanes = slice(h * DH, (h + 1) * DH)
            q = x[t, j + 1, 0, :, lanes]
            scores = [
                lax.dot_general(
                    q,
                    x[t, j + i, 1, :, lanes],
                    (((1,), (1,)), ((), ())),
                    preferred_element_type=jnp.float32,
                )
                * (DH ** (-0.5) * LOG2_E)
                + bias[j, :, i * rows : (i + 1) * rows]
                for i in range(2)
            ]
            top = jnp.max(jnp.maximum(scores[0], scores[1]), axis=-1, keepdims=True)
            powers = [jnp.exp2(s - top) for s in scores]
            total = jnp.sum(powers[0] + powers[1], axis=-1, keepdims=True)
            value = sum(
                jnp.dot(
                    powers[i].astype(jnp.bfloat16),
                    x[t, j + i, 2, :, lanes],
                    preferred_element_type=jnp.float32,
                )
                for i in range(2)
            )
            column = pl.multiple_of((2 * tp + t) * group + h * DH, DH)
            mixed[j, :, pl.ds(column, DH)] = (value / total).astype(jnp.bfloat16)

    def core_copy(t, j):
        part = mixed.at[j, :, pl.ds(pl.multiple_of((2 * tp + t) * group, DH), group)]
        return pltpu.make_async_remote_copy(
            src_ref=part,
            dst_ref=part,
            send_sem=core_send.at[t, j],
            recv_sem=core_recv.at[t, j],
            device_id=at(z, k, 1 - tp),
            device_id_type=MESH,
        )

    def relay(n):
        @pl.when(inner)
        def _():
            w_arrived(6 - 3 * z, n)
            w_relay(n).start()

    for t in range(2):
        x_own(t).wait()
        for m in (1, 2, 3):
            x_copy(t, m).wait_recv()

        @pl.when(z < LINE - 1)
        def _():
            halo_copy(t).start()

        relay(t)
        w_start(t + 2)

        @pl.loop(1, PLANE)
        def _(j):
            attend_rows(t, j)
            core_copy(t, j).start()

    relay(2)
    w_start(4)
    w_start(5)
    for t in range(2):
        @pl.when(z > 0)
        def _():
            halo_copy(t).wait_recv()

        attend_rows(t, 0)
        core_copy(t, 0).start()

    for t in range(2):
        for j in range(PLANE):
            core_copy(t, j).wait_recv()

    half = width // 2
    first = (1, 2)

    def give_copy(n, e):
        return pltpu.make_async_remote_copy(
            src_ref=give.at[n, e],
            dst_ref=take.at[n, e],
            send_sem=give_send.at[n, e],
            recv_sem=give_recv.at[n, e],
            device_id=at(z, mate(first[e])),
            device_id_type=MESH,
        )

    def pass_copy(n, e):
        return pltpu.make_async_remote_copy(
            src_ref=passed.at[n, e],
            dst_ref=landed.at[n, e],
            send_sem=pass_send.at[n, e],
            recv_sem=pass_recv.at[n, e],
            device_id=at(z, mate(3 - first[e])),
            device_id_type=MESH,
        )

    def multiply(n):
        w_own(n).wait()
        for zz in range(LINE):
            waited = jnp.logical_and(inner, 6 - 3 * z == zz)
            @pl.when(jnp.logical_and(z != zz, jnp.logical_not(waited)))
            def _():
                w_arrived(zz, n)

        def product(m, e):
            return jnp.dot(
                mixed[mate(m)],
                wv[:, n * width + e * half : n * width + (e + 1) * half],
                preferred_element_type=jnp.float32,
            )

        for e in range(2):
            give[n, e, 1] = product(3, e).astype(jnp.bfloat16)
            give[n, e, 0] = product(first[e], e).astype(jnp.bfloat16)
            give_copy(n, e).start()
        for e in range(2):
            later[n, e] = product(3 - first[e], e)
            kept[n, e] = product(0, e)

    def pass_on(n):
        for e in range(2):
            give_copy(n, e).wait_recv()
            passed[n, e] = (later[n, e] + take[n, e, 1].astype(jnp.float32)).astype(jnp.bfloat16)
            pass_copy(n, e).start()

    for n in range(CHUNKS):
        if n >= 3:
            relay(n)
        multiply(n)
        if n >= 2:
            pass_on(n - 2)
    pass_on(CHUNKS - 2)
    pass_on(CHUNKS - 1)

    def out_copy(n):
        return pltpu.make_async_copy(
            done.at[n], out.at[:, pl.ds(n * width, width)], out_sem.at[n]
        )

    for n in range(CHUNKS):
        for e in range(2):
            pass_copy(n, e).wait_recv()
            total = kept[n, e] + take[n, e, 0].astype(jnp.float32) + landed[n, e].astype(jnp.float32)
            done[n, :, e * half : (e + 1) * half] = total.astype(jnp.bfloat16)
        out_copy(n).start()

    for t in range(2):
        for m in (1, 2, 3):
            x_copy(t, m).wait_send()
        for j in range(PLANE):
            core_copy(t, j).wait_send()

        @pl.when(z < LINE - 1)
        def _():
            halo_copy(t).wait_send()

    for n in range(CHUNKS):
        for slot, step in w_steps:
            @pl.when(reaches(step))
            def _():
                w_copy(slot, step, n).wait_send()

        @pl.when(inner)
        def _():
            w_relay(n).wait_send()

        for e in range(2):
            give_copy(n, e).wait_send()
            pass_copy(n, e).wait_send()
        out_copy(n).wait()


def fused_shards(qkv, note_slot_document, note_rows, out_weight):
    rows, group = qkv.shape[1], out_weight.shape[0]
    columns = out_weight.shape[1]
    width = columns // CHUNKS
    dma = pltpu.SemaphoreType.DMA
    anywhere = pl.BlockSpec(memory_space=pl.ANY)
    scalars = pl.BlockSpec(memory_space=pltpu.SMEM)
    return pl.pallas_call(
        fused,
        out_shape=jax.ShapeDtypeStruct((rows, columns), jnp.bfloat16),
        in_specs=[scalars, scalars, anywhere, anywhere],
        out_specs=anywhere,
        scratch_shapes=[
            pltpu.VMEM((2, PLANE + 1, 3, rows, group), jnp.bfloat16),
            pltpu.VMEM((LINE * group, columns), jnp.bfloat16),
            pltpu.VMEM((PLANE, rows, LINE * group), jnp.bfloat16),
            pltpu.VMEM((PLANE, rows, 2 * rows), jnp.float32),
            pltpu.VMEM((CHUNKS, 2, 2, rows, width // 2), jnp.bfloat16),
            pltpu.VMEM((CHUNKS, 2, 2, rows, width // 2), jnp.bfloat16),
            pltpu.VMEM((CHUNKS, 2, rows, width // 2), jnp.bfloat16),
            pltpu.VMEM((CHUNKS, 2, rows, width // 2), jnp.bfloat16),
            pltpu.VMEM((CHUNKS, 2, rows, width // 2), jnp.float32),
            pltpu.VMEM((CHUNKS, 2, rows, width // 2), jnp.float32),
            pltpu.VMEM((CHUNKS, rows, width), jnp.bfloat16),
            dma((2, 4)), dma((2, 4)), dma((2,)), dma((2,)),
            dma((5, CHUNKS)), dma((LINE, CHUNKS)), dma((2, PLANE)), dma((2, PLANE)),
            dma((CHUNKS, 2)), dma((CHUNKS, 2)), dma((CHUNKS, 2)), dma((CHUNKS, 2)),
            dma((CHUNKS,)), dma((CHUNKS,)),
        ],
        compiler_params=pltpu.CompilerParams(
            collective_id=0, has_side_effects=True, vmem_limit_bytes=60 * 2**20
        ),
        cost_estimate=pl.CostEstimate(
            flops=2 * PLANE * rows * LINE * group * columns + 16 * rows * rows * DH * PLANE * 2 * group // DH,
            bytes_accessed=4 * (qkv.size + 3 * out_weight.size),
            transcendentals=PLANE * rows * 2 * rows * 2 * group // DH,
        ),
    )(note_slot_document, note_rows, qkv, out_weight)


def solution(mesh):
    in_specs = (P(None, "seg", "tp"), P(), P(), P("seg", "tp"))
    out_specs = P("seg", "tp")
    in_planes = mesh.shape["seg"] == PLANE * LINE and mesh.shape["tp"] == 2
    body = fused_shards if in_planes else shards
    return jax.shard_map(body, mesh=mesh, in_specs=in_specs, out_specs=out_specs, check_vma=False)
```

```python
import jax
import jax.numpy as jnp
from jax import lax
from jax.experimental import pallas as pl
from jax.experimental.pallas import tpu as pltpu
from jax.sharding import PartitionSpec as P

DH = 128
NOTE_BLOCK_ROWS = 128


masked_score = -1e30


def from_behind(x, axis, by):
    length = lax.axis_size(axis)
    pairs = [(i, i + by) for i in range(length) if 0 <= i + by < length]
    return lax.ppermute(x, axis, pairs)


def attend(queries, key_rows, value_rows, query_doc, key_doc):
    scores = jnp.einsum(
        "qhd,khd->hqk", queries, key_rows, preferred_element_type=jnp.float32
    ) * DH ** (-0.5)
    scores = jnp.where((query_doc[:, None] == key_doc[None, :])[None], scores, masked_score)
    row_max = jnp.max(scores, axis=-1, keepdims=True)
    exponent = jnp.exp(scores - row_max)
    weights = (exponent / jnp.sum(exponent, axis=-1, keepdims=True)).astype(jnp.bfloat16)
    mixed = jnp.einsum("hqk,khd->qhd", weights, value_rows, preferred_element_type=jnp.float32)
    return mixed.astype(jnp.bfloat16)


def attend_blocks(queries, key_rows, value_rows, row_docs, key_doc):
    row_count, head_count = (queries.shape[0], queries.shape[1])
    block_rows = min(row_count, 512)
    block_count = row_count // block_rows

    def one_block(query_pair):
        return attend(query_pair[0], key_rows, value_rows, query_pair[1], key_doc)

    mixed = lax.map(
        one_block,
        (
            queries.reshape(block_count, block_rows, head_count, DH),
            row_docs.reshape(block_count, block_rows),
        ),
    )
    return mixed.reshape(row_count, head_count * DH)


def shards(qkv, note_slot_document, note_rows, out_weight):
    row_count = qkv.shape[1]
    head_count = qkv.shape[2] // DH
    slot_count = row_count // NOTE_BLOCK_ROWS
    seg_place = lax.axis_index("seg")
    memory = from_behind(qkv[1:], "seg", 1)
    slot_docs = lax.dynamic_slice_in_dim(note_slot_document, seg_place * slot_count, slot_count)
    slot_live = lax.dynamic_slice_in_dim(note_rows, seg_place * slot_count, slot_count)
    past_first = jnp.maximum(seg_place - 1, 0) * slot_count
    past_docs = jnp.where(
        seg_place > 0, lax.dynamic_slice_in_dim(note_slot_document, past_first, slot_count), -1
    )
    past_live = lax.dynamic_slice_in_dim(note_rows, past_first, slot_count)
    inside_note_block = jnp.arange(row_count) % NOTE_BLOCK_ROWS
    row_docs = jnp.repeat(slot_docs, NOTE_BLOCK_ROWS)
    own_doc = jnp.where(inside_note_block < jnp.repeat(slot_live, NOTE_BLOCK_ROWS), row_docs, -2)
    earlier_document = jnp.where(
        inside_note_block < jnp.repeat(past_live, NOTE_BLOCK_ROWS),
        jnp.repeat(past_docs, NOTE_BLOCK_ROWS),
        -2,
    )
    queries = qkv[0].reshape(row_count, head_count, DH)
    own_keys = qkv[1].reshape(row_count, head_count, DH)
    own_values = qkv[2].reshape(row_count, head_count, DH)
    key_rows = jnp.concatenate([memory[0].reshape(row_count, head_count, DH), own_keys], axis=0)
    value_rows = jnp.concatenate([memory[1].reshape(row_count, head_count, DH), own_values], axis=0)
    mixed_heads = attend_blocks(
        queries, key_rows, value_rows, row_docs, jnp.concatenate([earlier_document, own_doc])
    )
    heads_all = lax.all_gather(mixed_heads, "tp", axis=1, tiled=True)
    summed = jnp.dot(
        heads_all,
        lax.all_gather(out_weight, "seg", axis=0, tiled=True),
        preferred_element_type=jnp.float32,
    )
    return summed.astype(jnp.bfloat16)


PLANE = 4
LINE = 4
CHUNKS = 6
LOG2_E = 1.4426950408889634
MESH = pl.DeviceIdType.MESH


def fused(
    docs, live, qkv, w, out, x, wv, mixed, bias, give, take, passed, landed, kept, later, done,
    x_send, x_recv, halo_send, halo_recv, w_send, w_recv, core_send, core_recv,
    give_send, give_recv, pass_send, pass_recv, own_sem, out_sem,
):
    seg, tp = lax.axis_index("seg"), lax.axis_index("tp")
    z, k = seg // PLANE, seg % PLANE
    kx, ky = k % 2, k // 2
    rows = qkv.shape[1]
    width = w.shape[1] // CHUNKS
    group = w.shape[0]
    heads = group // DH
    slots = rows // NOTE_BLOCK_ROWS
    inner = jnp.logical_and(z > 0, z < LINE - 1)
    pieces = 2 * heads

    def mate(m):
        px = 1 - kx if m in (1, 3) else kx
        py = 1 - ky if m in (2, 3) else ky
        return 2 * py + px

    def at(zz, kk, cc=None):
        return (zz * PLANE + kk, tp if cc is None else cc)

    barrier = pltpu.get_barrier_semaphore()
    peers = [at(z, mate(m)) for m in (1, 2, 3)]
    peers += [at((z + d) % LINE, k) for d in (1, 2, 3)] + [at(z, k, 1 - tp)]
    for peer in peers:
        pl.semaphore_signal(barrier, inc=1, device_id=peer, device_id_type=MESH)
    pl.semaphore_wait(barrier, len(peers))

    def piece_lanes(t, kk):
        start = (PLANE * (t // heads) + kk) * group + t % heads * DH
        return pl.ds(pl.multiple_of(start, DH), DH)

    def x_copy(t, m):
        return pltpu.make_async_remote_copy(
            src_ref=qkv.at[:, :, piece_lanes(t, mate(m))],
            dst_ref=x.at[t, k + 1],
            send_sem=x_send.at[t, m],
            recv_sem=x_recv.at[t, m],
            device_id=at(z, mate(m)),
            device_id_type=MESH,
        )

    def x_own(t):
        return pltpu.make_async_copy(
            qkv.at[:, :, piece_lanes(t, k)],
            x.at[t, k + 1],
            x_recv.at[t, 0],
        )

    def halo_copy(t):
        return pltpu.make_async_remote_copy(
            src_ref=x.at[t, PLANE, pl.ds(1, 2)],
            dst_ref=x.at[t, 0, pl.ds(1, 2)],
            send_sem=halo_send.at[t],
            recv_sem=halo_recv.at[t],
            device_id=at(jnp.minimum(z + 1, LINE - 1), k),
            device_id_type=MESH,
        )

    def w_block(zz, n):
        return wv.at[pl.ds(pl.multiple_of(zz * group, DH), group), pl.ds(n * width, width)]

    def w_copy(slot, step, n):
        return pltpu.make_async_remote_copy(
            src_ref=w.at[:, pl.ds(n * width, width)],
            dst_ref=w_block(z, n),
            send_sem=w_send.at[slot, n],
            recv_sem=w_recv.at[z, n],
            device_id=at(z + step, k),
            device_id_type=MESH,
        )

    def w_relay(n):
        far = 6 - 3 * z
        return pltpu.make_async_remote_copy(
            src_ref=w_block(far, n),
            dst_ref=w_block(far, n),
            send_sem=w_send.at[4, n],
            recv_sem=w_recv.at[far, n],
            device_id=at(3 * z - 3, k),
            device_id_type=MESH,
        )

    def w_own(n):
        return pltpu.make_async_copy(
            w.at[:, pl.ds(n * width, width)], w_block(z, n), own_sem.at[n]
        )

    def w_arrived(zz, n):
        pltpu.make_async_copy(w_block(zz, n), w_block(zz, n), w_recv.at[zz, n]).wait()

    w_steps = ((0, 2), (1, -2), (2, 1), (3, -1))

    def reaches(step):
        return z < LINE - step if step > 0 else z >= -step

    for t in range(pieces):
        for m in (3, 1, 2):
            x_copy(t, m).start()
        x_own(t).start()

    def w_start(n, way):
        for slot, step in w_steps:
            if step * way > 0:
                go = reaches(step)
                if abs(step) == 2 and n > 1:
                    go = jnp.logical_and(go, inner)
                @pl.when(go)
                def _():
                    w_copy(slot, step, n).start()

    for n in range(2):
        w_start(n, 1)
        w_start(n, -1)
    for n in range(2, CHUNKS):
        for slot, step in w_steps[:2]:
            @pl.when(jnp.logical_and(reaches(step), jnp.logical_not(inner)))
            def _():
                w_copy(slot, step, n).start()
    w_start(2, -1)
    for n in range(CHUNKS):
        w_own(n).start()

    @pl.when(z == 0)
    def _():
        for t in range(pieces):
            x[t, 0, 1:3] = jnp.zeros((2, rows, DH), x.dtype)

    place = lax.broadcasted_iota(jnp.int32, (NOTE_BLOCK_ROWS, NOTE_BLOCK_ROWS), 1)

    @pl.loop(0, PLANE)
    def _(j):
        first = (z * PLANE + j) * slots
        for a in range(slots):
            for b in range(2 * slots):
                key_slot = first + b - slots
                safe = jnp.maximum(key_slot, 0)
                same = jnp.logical_and(docs[safe] == docs[first + a], key_slot >= 0)
                limit = jnp.where(same, live[safe], 0)
                bias[
                    j,
                    a * NOTE_BLOCK_ROWS : (a + 1) * NOTE_BLOCK_ROWS,
                    b * NOTE_BLOCK_ROWS : (b + 1) * NOTE_BLOCK_ROWS,
                ] = jnp.where(place < limit, 0.0, masked_score)

    def attend_rows(t, j):
        scores = [
            lax.dot_general(
                x[t, j + 1, 0],
                x[t, j + i, 1],
                (((1,), (1,)), ((), ())),
                preferred_element_type=jnp.float32,
            )
            * (DH ** (-0.5) * LOG2_E)
            + bias[j, :, i * rows : (i + 1) * rows]
            for i in range(2)
        ]
        top = jnp.max(jnp.maximum(scores[0], scores[1]), axis=-1, keepdims=True)
        powers = [jnp.exp2(s - top) for s in scores]
        total = jnp.sum(powers[0] + powers[1], axis=-1, keepdims=True)
        value = sum(
            jnp.dot(
                powers[i].astype(jnp.bfloat16), x[t, j + i, 2], preferred_element_type=jnp.float32
            )
            for i in range(2)
        )
        column = pl.multiple_of((2 * tp + t // heads) * group + t % heads * DH, DH)
        mixed[j, :, pl.ds(column, DH)] = (value / total).astype(jnp.bfloat16)

    def core_copy(t, j):
        part = mixed.at[j, :, pl.ds(pl.multiple_of((2 * tp + t) * group, DH), group)]
        return pltpu.make_async_remote_copy(
            src_ref=part,
            dst_ref=part,
            send_sem=core_send.at[t, j],
            recv_sem=core_recv.at[t, j],
            device_id=at(z, k, 1 - tp),
            device_id_type=MESH,
        )

    def relay(n):
        @pl.when(inner)
        def _():
            w_arrived(6 - 3 * z, n)
            w_relay(n).start()

    for t in range(pieces):
        x_own(t).wait()
        for m in (1, 2, 3):
            x_copy(t, m).wait_recv()

        @pl.when(z < LINE - 1)
        def _():
            halo_copy(t).start()

        if t == pieces // 2 - 1:
            w_start(2, 1)
            w_start(3, -1)
        if t == pieces - 1:
            for n in range(3, CHUNKS):
                w_start(n, 1)
                if n > 3:
                    w_start(n, -1)
        if t >= pieces - 4:
            relay(t - pieces + 4)

        @pl.loop(1, PLANE)
        def _(j):
            attend_rows(t, j)
            if t % heads == heads - 1:
                core_copy(t // heads, j).start()

    for t in range(pieces):
        @pl.when(z > 0)
        def _():
            halo_copy(t).wait_recv()

        attend_rows(t, 0)
        if t % heads == heads - 1:
            core_copy(t // heads, 0).start()
    relay(4)

    for t in range(2):
        for j in range(PLANE):
            core_copy(t, j).wait_recv()

    half = width // 2
    first = (1, 2)

    def give_copy(n, e):
        return pltpu.make_async_remote_copy(
            src_ref=give.at[n, e],
            dst_ref=take.at[n, e],
            send_sem=give_send.at[n, e],
            recv_sem=give_recv.at[n, e],
            device_id=at(z, mate(first[e])),
            device_id_type=MESH,
        )

    def pass_copy(n, e):
        return pltpu.make_async_remote_copy(
            src_ref=passed.at[n, e],
            dst_ref=landed.at[n, e],
            send_sem=pass_send.at[n, e],
            recv_sem=pass_recv.at[n, e],
            device_id=at(z, mate(3 - first[e])),
            device_id_type=MESH,
        )

    def multiply(n):
        w_own(n).wait()
        for zz in range(LINE):
            waited = jnp.logical_and(inner, 6 - 3 * z == zz)
            @pl.when(jnp.logical_and(z != zz, jnp.logical_not(waited)))
            def _():
                w_arrived(zz, n)

        def product(m, e):
            return jnp.dot(
                mixed[mate(m)],
                wv[:, n * width + e * half : n * width + (e + 1) * half],
                preferred_element_type=jnp.float32,
            )

        for e in range(2):
            give[n, e, 1] = product(3, e).astype(jnp.bfloat16)
            give[n, e, 0] = product(first[e], e).astype(jnp.bfloat16)
            give_copy(n, e).start()
        for e in range(2):
            later[n, e] = product(3 - first[e], e)
            kept[n, e] = product(0, e)

    def pass_on(n):
        for e in range(2):
            give_copy(n, e).wait_recv()
            passed[n, e] = (later[n, e] + take[n, e, 1].astype(jnp.float32)).astype(jnp.bfloat16)
            pass_copy(n, e).start()

    for n in range(CHUNKS):
        if n == 1:
            relay(CHUNKS - 1)
        multiply(n)
        if n >= 2:
            pass_on(n - 2)
    pass_on(CHUNKS - 2)
    pass_on(CHUNKS - 1)

    def out_copy(n):
        return pltpu.make_async_copy(
            done.at[n], out.at[:, pl.ds(n * width, width)], out_sem.at[n]
        )

    for n in range(CHUNKS):
        for e in range(2):
            pass_copy(n, e).wait_recv()
            total = kept[n, e] + take[n, e, 0].astype(jnp.float32) + landed[n, e].astype(jnp.float32)
            done[n, :, e * half : (e + 1) * half] = total.astype(jnp.bfloat16)
        out_copy(n).start()

    for t in range(2):
        for j in range(PLANE):
            core_copy(t, j).wait_send()

    for t in range(pieces):
        for m in (1, 2, 3):
            x_copy(t, m).wait_send()

        @pl.when(z < LINE - 1)
        def _():
            halo_copy(t).wait_send()

    for n in range(CHUNKS):
        for slot, step in w_steps:
            @pl.when(reaches(step))
            def _():
                w_copy(slot, step, n).wait_send()

        @pl.when(inner)
        def _():
            w_relay(n).wait_send()

        for e in range(2):
            give_copy(n, e).wait_send()
            pass_copy(n, e).wait_send()
        out_copy(n).wait()


def fused_shards(qkv, note_slot_document, note_rows, out_weight):
    rows, group = qkv.shape[1], out_weight.shape[0]
    columns = out_weight.shape[1]
    width = columns // CHUNKS
    pieces = 2 * group // DH
    dma = pltpu.SemaphoreType.DMA
    anywhere = pl.BlockSpec(memory_space=pl.ANY)
    scalars = pl.BlockSpec(memory_space=pltpu.SMEM)
    return pl.pallas_call(
        fused,
        out_shape=jax.ShapeDtypeStruct((rows, columns), jnp.bfloat16),
        in_specs=[scalars, scalars, anywhere, anywhere],
        out_specs=anywhere,
        scratch_shapes=[
            pltpu.VMEM((pieces, PLANE + 1, 3, rows, DH), jnp.bfloat16),
            pltpu.VMEM((LINE * group, columns), jnp.bfloat16),
            pltpu.VMEM((PLANE, rows, LINE * group), jnp.bfloat16),
            pltpu.VMEM((PLANE, rows, 2 * rows), jnp.float32),
            pltpu.VMEM((CHUNKS, 2, 2, rows, width // 2), jnp.bfloat16),
            pltpu.VMEM((CHUNKS, 2, 2, rows, width // 2), jnp.bfloat16),
            pltpu.VMEM((CHUNKS, 2, rows, width // 2), jnp.bfloat16),
            pltpu.VMEM((CHUNKS, 2, rows, width // 2), jnp.bfloat16),
            pltpu.VMEM((CHUNKS, 2, rows, width // 2), jnp.float32),
            pltpu.VMEM((CHUNKS, 2, rows, width // 2), jnp.float32),
            pltpu.VMEM((CHUNKS, rows, width), jnp.bfloat16),
            dma((pieces, 4)), dma((pieces, 4)), dma((pieces,)), dma((pieces,)),
            dma((5, CHUNKS)), dma((LINE, CHUNKS)), dma((2, PLANE)), dma((2, PLANE)),
            dma((CHUNKS, 2)), dma((CHUNKS, 2)), dma((CHUNKS, 2)), dma((CHUNKS, 2)),
            dma((CHUNKS,)), dma((CHUNKS,)),
        ],
        compiler_params=pltpu.CompilerParams(
            collective_id=0, has_side_effects=True, vmem_limit_bytes=60 * 2**20
        ),
        cost_estimate=pl.CostEstimate(
            flops=2 * PLANE * rows * LINE * group * columns + 16 * rows * rows * DH * PLANE * 2 * group // DH,
            bytes_accessed=4 * (qkv.size + 3 * out_weight.size),
            transcendentals=PLANE * rows * 2 * rows * 2 * group // DH,
        ),
    )(note_slot_document, note_rows, qkv, out_weight)


def solution(mesh):
    in_specs = (P(None, "seg", "tp"), P(), P(), P("seg", "tp"))
    out_specs = P("seg", "tp")
    in_planes = mesh.shape["seg"] == PLANE * LINE and mesh.shape["tp"] == 2
    body = fused_shards if in_planes else shards
    return jax.shard_map(body, mesh=mesh, in_specs=in_specs, out_specs=out_specs, check_vma=False)
```
